256 devices in a mesh: row: 16 (over y, z_hi), col: 16 (over x, z_lo, core).
Axes of the slice: x: 4, y: 4, z: 8 (z_hi: 4, z_lo: 2; z = z_hi * 2 + z_lo), core: 2. Of those that a mesh axis runs over, the one named last changes fastest.
Arguments:
- object_field: float32 [2, 6144, 6144], P(None, 'row', 'col'), may hold values from -6 to 6
- probe: float32 [4, 2, 128, 128], replicated, may hold values from -6 to 6
- positions: int32 [16, 16, 8, 2], P('row', 'col'), may hold values from 0 to 383
- counts: int32 [16, 16], P('row', 'col'), may hold values from 4 to 8, as said below
- measured: float32 [16, 16, 8, 128, 128], P('row', 'col'), may hold values from 0 to 3
Outputs:
- object_grad: float32 [2, 6144, 6144], P(None, 'row', 'col')
- probe_grad: float32 [4, 2, 128, 128], replicated
The draws below stay inside these ranges and needn't reach their ends.
Inputs may be any that keep to these rules, and one draw needn't show every extreme that they name: `counts`: devices in the first or last index of either axis hold between 4 and 8 live slots; all other devices hold 8.
All inputs are finite; a program needn't handle non-finite values.
Results may differ from the reference program's by a relative error of at most 0.00016.
Values sent between devices are 32-bit elements; how exact they have to be, the bound alone decides.
A program may use at most 64 MiB of HBM per device.

```python
import jax
import jax.numpy as jnp
from jax import lax

PATTERN_PIXELS = 128
M = 4
TILE = 384
P_SIZE = 8
H = 6144
W = 6144
N_ROW = 16
N_COL = 16


def draw_counts(key, part):
    key = jax.random.fold_in(key, 11)
    rows_idx = jnp.arange(N_ROW, dtype=jnp.int32)[:, None] + jnp.zeros((N_ROW, N_COL), jnp.int32)
    cols_idx = jnp.arange(N_COL, dtype=jnp.int32)[None, :] + jnp.zeros((N_ROW, N_COL), jnp.int32)
    border = (rows_idx == 0) | (rows_idx == N_ROW - 1) | (cols_idx == 0) | (cols_idx == N_COL - 1)
    lower = jax.random.randint(key, (N_ROW, N_COL), P_SIZE // 2, P_SIZE + 1, dtype=jnp.int32)
    return jnp.where(border, lower, P_SIZE).astype(jnp.int32)


def set_ends(values, rng, least, largest):
    extent = values.shape
    spot = [jax.random.randint(jax.random.fold_in(rng, axis), (), 0, extent[axis]) for axis in range(len(extent))]
    values = values.at[tuple(spot)].set(least)
    longest = extent.index(max(extent))
    spot[longest] = (spot[longest] + 1) % extent[longest]
    return values.at[tuple(spot)].set(largest)


def steps_of(stream_key, extent, split, smallest, largest):
    loudness = 1.0
    for dim, shards_of in split:
        draws = jax.random.uniform(jax.random.fold_in(jax.random.fold_in(stream_key, 6), dim), (shards_of,), jnp.float32, smallest / len(split), largest / len(split))
        loudness = loudness * jnp.repeat(jnp.exp(draws), extent[dim] // shards_of).reshape((-1,) + (1,) * (len(extent) - 1 - dim))
    return loudness


def normal_values(stream_key, dims, deviation, reach, pieces=(), kind=jnp.bfloat16):
    factor_of = steps_of(stream_key, dims, pieces, -0.22, 0.18) if pieces else 1.0
    array = jax.random.normal(stream_key, dims, jnp.float32) * deviation * factor_of
    return jnp.minimum(jnp.maximum(array, -reach), reach).astype(kind)


def setup_inputs(seed: int = 0) -> dict:
    streams_of = jax.random.split(jax.random.key(seed), 6)
    return {
        "object_field": normal_values(streams_of[0], (2, H, W), 0.7, 6.0, ((1, 16), (2, 16)), jnp.float32),
        "probe": normal_values(streams_of[1], (M, 2, PATTERN_PIXELS, PATTERN_PIXELS), 0.5, 6.0, (), jnp.float32),
        "positions": set_ends(jax.random.randint(streams_of[2], (N_ROW, N_COL, P_SIZE, 2), 0, TILE), jax.random.fold_in(streams_of[2], 1), 0, TILE - 1).astype(jnp.int32),
        "counts": draw_counts(jax.random.fold_in(streams_of[5], 71), 0),
        "measured": jnp.clip(3.0 * jax.random.uniform(streams_of[4], (N_ROW, N_COL, P_SIZE, PATTERN_PIXELS, PATTERN_PIXELS), jnp.float32) ** steps_of(streams_of[4], (N_ROW, N_COL, P_SIZE, PATTERN_PIXELS, PATTERN_PIXELS), ((0, 16), (1, 16)), -0.2, 0.2), 0.0, 3.0),
    }


def reference(object_field, probe, positions, counts, measured):
    half_width = PATTERN_PIXELS // 2
    padded = jnp.pad(object_field, ((0, 0), (half_width, half_width), (half_width, half_width)))
    probe_c = probe[:, 0] + 1j * probe[:, 1]
    accumulated_loss = N_ROW * N_COL * P_SIZE
    flat_pos = positions.reshape(accumulated_loss, 2)
    flattened_measurement = measured.reshape(accumulated_loss, PATTERN_PIXELS, PATTERN_PIXELS)
    index_all = jnp.arange(accumulated_loss, dtype=jnp.int32)
    dev_row = index_all // (N_COL * P_SIZE)
    dev_col = index_all // P_SIZE % N_COL
    slot_of = index_all % P_SIZE
    active_flag = (slot_of < counts[dev_row, dev_col]).astype(jnp.float32)
    row_location = (dev_row * TILE + flat_pos[:, 0]).astype(jnp.int32)
    column_location = (dev_col * TILE + flat_pos[:, 1]).astype(jnp.int32)

    def scan_iteration(running, scan_record):
        gradient_margined, probe_accumulator = running
        row_current, column_current, measured_amplitude, active_current = scan_record
        zero_idx = jnp.int32(0)
        patch = lax.dynamic_slice(padded, (zero_idx, row_current, column_current), (2, PATTERN_PIXELS, PATTERN_PIXELS))
        obj_c = patch[0] + 1j * patch[1]
        exit_wave = probe_c * obj_c
        farfield = jnp.fft.fft2(exit_wave, norm='ortho')
        intensity = lax.optimization_barrier(jnp.sum(jnp.real(farfield) ** 2 + jnp.imag(farfield) ** 2, axis=0))
        predicted_amplitude = jnp.sqrt(intensity + 0.1)
        amplitude_ratio = (1.0 - measured_amplitude / predicted_amplitude) * active_current
        back = jnp.fft.ifft2(amplitude_ratio * farfield, norm='ortho')
        obj_g = lax.optimization_barrier(jnp.sum(jnp.conj(probe_c) * back, axis=0))
        probe_g = jnp.conj(obj_c) * back
        current = lax.dynamic_slice(gradient_margined, (zero_idx, row_current, column_current), (2, PATTERN_PIXELS, PATTERN_PIXELS))
        updated = current + jnp.stack([jnp.real(obj_g), jnp.imag(obj_g)], axis=0)
        gradient_margined = lax.dynamic_update_slice(gradient_margined, updated, (zero_idx, row_current, column_current))
        probe_accumulator = probe_accumulator + jnp.stack([jnp.real(probe_g), jnp.imag(probe_g)], axis=1)
        return ((gradient_margined, probe_accumulator), None)
    initial_state = (jnp.zeros(padded.shape, jnp.float32), jnp.zeros(probe.shape, jnp.float32))
    (gradient_margined, probe_accumulator), unused_slot = lax.scan(scan_iteration, initial_state, (row_location, column_location, flattened_measurement, active_flag))
    object_grad = gradient_margined[:, half_width:-half_width, half_width:-half_width]
    return (object_grad, probe_accumulator / jnp.sqrt(jnp.float32(accumulated_loss)))
```

```python
import functools
import math

import jax
import jax.numpy as jnp
import numpy as np
from jax import lax
from jax.experimental import pallas as pl
from jax.experimental.pallas import tpu as pltpu
from jax.sharding import PartitionSpec as P

MESH = pl.DeviceIdType.MESH
ANY = pl.BlockSpec(memory_space=pl.ANY)
VMEM = pl.BlockSpec(memory_space=pltpu.VMEM)
SMEM = pl.BlockSpec(memory_space=pltpu.SMEM)
F32 = jnp.float32
BF16 = jnp.bfloat16
N = 128
HALF = 64
SIDES = ((-1, 0), (1, 0), (0, -1), (0, 1), (-1, -1), (-1, 1), (1, -1), (1, 1))
OPPOSITE = tuple(SIDES.index((-a, -b)) for a, b in SIDES)


def neighbours(rows, cols):
    r, c = lax.axis_index("row"), lax.axis_index("col")
    out = []
    for dr, dc in SIDES:
        there = True
        if dr:
            there = (r > 0) if dr < 0 else (r < rows - 1)
        if dc:
            col_there = (c > 0) if dc < 0 else (c < cols - 1)
            there = col_there if there is True else jnp.logical_and(there, col_there)
        out.append((there, (r + dr, c + dc)))
    return out


def rim_barrier(near):
    barrier = pltpu.get_barrier_semaphore()
    for there, device in near:
        @pl.when(there)
        def _():
            pl.semaphore_signal(barrier, inc=1, device_id=device, device_id_type=MESH)
    pl.semaphore_wait(barrier, sum(there.astype(jnp.int32) for there, _ in near))


def pack_low(tile):
    k = tile.shape[1] // 2
    lane = lax.broadcasted_iota(jnp.int32, (2, k, N), 2)
    return jnp.where(lane < HALF, tile[:, :k], pltpu.roll(tile[:, k:], HALF, 2))


def pack_high(tile):
    k = tile.shape[1] // 2
    lane = lax.broadcasted_iota(jnp.int32, (2, k, N), 2)
    return jnp.where(lane < HALF, pltpu.roll(tile[:, :k], HALF, 2), tile[:, k:])


def halo_kernel(rows, cols, obj, top, bot, left, right, c0, c1, c2, c3,
                tiles, packed, packed_c, load_sem, send_sem, recv_sem):
    near = neighbours(rows, cols)
    size = obj.shape[1]
    loads = [
        pltpu.make_async_copy(obj.at[:, :, pl.ds(lane, N)], tiles.at[i], load_sem.at[i])
        for i, lane in enumerate((0, size - N))
    ]
    for load in loads:
        load.start()
    rim_barrier(near)
    landing = (top, bot, left, right, c0, c1, c2, c3)
    sources = [obj.at[:, pl.ds(0, HALF), :], obj.at[:, pl.ds(size - HALF, HALF), :],
               packed.at[0], packed.at[1]] + [packed_c.at[i] for i in range(4)]
    copies = []
    for side in range(8):
        copies.append(pltpu.make_async_remote_copy(
            src_ref=sources[side], dst_ref=landing[OPPOSITE[side]],
            send_sem=send_sem.at[side], recv_sem=recv_sem.at[OPPOSITE[side]],
            device_id=near[side][1], device_id_type=MESH))

    def start(side):
        @pl.when(near[side][0])
        def _():
            copies[side].start()

    start(0)
    start(1)
    loads[0].wait()
    packed[0] = pack_low(tiles[0])
    start(2)
    loads[1].wait()
    packed[1] = pack_high(tiles[1])
    start(3)
    packed_c[0] = pack_low(tiles[0, :, :HALF])
    packed_c[1] = pack_high(tiles[1, :, :HALF])
    packed_c[2] = pack_low(tiles[0, :, size - HALF:])
    packed_c[3] = pack_high(tiles[1, :, size - HALF:])
    for side in range(4, 8):
        start(side)
    for side in range(8):
        @pl.when(near[side][0])
        def _():
            copies[side].wait_send()
            copies[OPPOSITE[side]].wait_recv()


def exchange_halo(obj, rows, cols):
    size = obj.shape[1]
    row_strip = jax.ShapeDtypeStruct((2, HALF, size), F32)
    col_strip = jax.ShapeDtypeStruct((2, size // 2, N), F32)
    corner = jax.ShapeDtypeStruct((2, HALF // 2, N), F32)
    return pl.pallas_call(
        functools.partial(halo_kernel, rows, cols),
        out_shape=[row_strip] * 2 + [col_strip] * 2 + [corner] * 4,
        in_specs=[ANY],
        out_specs=[ANY] * 8,
        scratch_shapes=[
            pltpu.VMEM((2, 2, size, N), F32),
            pltpu.VMEM((2, 2, size // 2, N), F32),
            pltpu.VMEM((4, 2, HALF // 2, N), F32),
            pltpu.SemaphoreType.DMA((2,)),
            pltpu.SemaphoreType.DMA((8,)),
            pltpu.SemaphoreType.DMA((8,)),
        ],
        compiler_params=pltpu.CompilerParams(collective_id=0, has_side_effects=True),
        name="halo",
    )(obj)


def tables():
    ramp = np.arange(N)
    angles = 2.0 * math.pi / N * (ramp[:, None] * ramp[None, :] % N)
    cos, sin = np.cos(angles) / math.sqrt(N), np.sin(angles) / math.sqrt(N)
    minus = np.block([[cos, -sin], [sin, cos]]).astype(np.float32)
    high = minus.astype(jnp.bfloat16)
    low = (minus - high.astype(np.float32)).astype(jnp.bfloat16)
    plus_high, plus_low = np.ascontiguousarray(high.T), np.ascontiguousarray(low.T)
    return np.stack([high, low, plus_high, plus_low])


def split(x):
    high = x.astype(BF16)
    return high, (x - high.astype(F32)).astype(BF16)


def dot(a, b):
    return jnp.dot(a, b, preferred_element_type=F32)


def times_table(x, high, low):
    x_high, x_low = split(x)
    return dot(x_high, high) + (dot(x_low, high) + dot(x_high, low))


def table_times(high, low, x):
    x_high, x_low = split(x)
    return dot(high, x_high) + (dot(high, x_low) + dot(low, x_high))


def compute_kernel(rows, cols, pos, count, obj, top, bot, left, right, c0, c1, c2, c3, probe, measured, table,
                   center, up, down, pack_l, pack_r, k0, k1, k2, k3, probe_grad,
                   ext, grad, strips, corners, sem):
    modes, slots = probe.shape[0], measured.shape[0]
    size = center.shape[1]
    r, c = lax.axis_index("row"), lax.axis_index("col")
    here = ((r > 0), (r < rows - 1), (c > 0), (c < cols - 1))
    both = jnp.logical_and
    here = here + (both(here[0], here[2]), both(here[0], here[3]), both(here[1], here[2]), both(here[1], here[3]))
    low_edge, high_edge = HALF + size, N + size
    sources = (top, bot, left, right, c0, c1, c2, c3)
    targets = (
        ext.at[:, pl.ds(0, HALF // 8), :, pl.ds(N, size)],
        ext.at[:, pl.ds(low_edge // 8, HALF // 8), :, pl.ds(N, size)],
        strips.at[0], strips.at[1]) + tuple(corners.at[i] for i in range(4))
    copies = [pltpu.make_async_copy(s, t, sem.at[i]) for i, (s, t) in enumerate(zip(sources, targets))]
    whole = pltpu.make_async_copy(obj, ext.at[:, pl.ds(HALF // 8, size // 8), :, pl.ds(N, size)], sem.at[8])
    whole.start()
    for side in range(8):
        @pl.when(here[side])
        def _():
            copies[side].start()

        @pl.when(jnp.logical_not(here[side]))
        def _():
            targets[side][...] = jnp.zeros(targets[side].shape, F32)
    grad[...] = jnp.zeros_like(grad)
    probe_grad[...] = jnp.zeros_like(probe_grad)
    for side in range(8):
        @pl.when(here[side])
        def _():
            copies[side].wait()

    def unpack(packed, row, lane, is_low):
        k, row = packed.shape[1] // 8, row // 8
        turned = pltpu.roll(packed, HALF, 2)
        first, second = (packed, turned) if is_low else (turned, packed)
        ext[:, row:row + k, :, lane:lane + N] = first.reshape(2, k, 8, N)
        ext[:, row + k:row + 2 * k, :, lane:lane + N] = second.reshape(2, k, 8, N)

    unpack(strips[0], HALF, 0, False)
    unpack(strips[1], HALF, high_edge, True)
    unpack(corners[0], 0, 0, False)
    unpack(corners[1], 0, high_edge, True)
    unpack(corners[2], low_edge, 0, False)
    unpack(corners[3], low_edge, high_edge, True)
    whole.wait()

    minus_high, minus_low, plus_high, plus_low = (table[i] for i in range(4))
    groups = N // 8
    lane = lax.broadcasted_iota(jnp.int32, (groups + 1, 8, N), 2)
    step = lax.broadcasted_iota(jnp.int32, (groups + 1, 8, N), 1)
    live = count[0, 0]

    def one_slot(slot, carry):
        row = pos[0, 0, slot, 0]
        group, down_by = row // 8, row % 8
        col = pos[0, 0, slot, 1] + HALF
        first = pl.multiple_of(col // N * N, N)
        second = pl.multiple_of(first + N, N)
        shift = col % N
        back = (N - shift) % N
        kept = lane >= shift

        def cut(part):
            a = ext[part, pl.ds(group, groups + 1), :, pl.ds(first, N)]
            b = ext[part, pl.ds(group, groups + 1), :, pl.ds(second, N)]
            x = pltpu.roll(jnp.where(kept, a, b), back, 2)
            x = pltpu.roll(x, (8 - down_by) % 8, 1)
            return jnp.where(step[:groups] < 8 - down_by, x[:groups], x[1:]).reshape(N, N)

        p_re, p_im = cut(0), cut(1)
        waves = []
        for m in range(modes):
            q_re, q_im = probe[m, 0], probe[m, 1]
            waves.append(jnp.concatenate([q_re * p_re - q_im * p_im, q_re * p_im + q_im * p_re], axis=1))
        half = times_table(jnp.concatenate(waves, axis=0), minus_high, minus_low)
        half = jnp.concatenate(
            [jnp.concatenate([half[m * N:(m + 1) * N, :N], half[m * N:(m + 1) * N, N:]], axis=0)
             for m in range(modes)], axis=1)
        far = table_times(plus_high, plus_low, half)
        power = far[:N] * far[:N] + far[N:] * far[N:]
        intensity = sum(power[:, m * N:(m + 1) * N] for m in range(modes))
        alive = jnp.where(slot < live, 1.0, 0.0).astype(F32)
        factor = (1.0 - measured[slot] * lax.rsqrt(intensity + 0.1)) * alive
        wide = jnp.concatenate([factor] * modes, axis=1)
        far = far * jnp.concatenate([wide, wide], axis=0)
        half = table_times(minus_high, minus_low, far)
        half = jnp.concatenate(
            [jnp.concatenate([half[:N, m * N:(m + 1) * N], half[N:, m * N:(m + 1) * N]], axis=1)
             for m in range(modes)], axis=0)
        g = times_table(half, plus_high, plus_low)
        o_re = jnp.zeros((N, N), F32)
        o_im = jnp.zeros((N, N), F32)
        for m in range(modes):
            g_re, g_im = g[m * N:(m + 1) * N, :N], g[m * N:(m + 1) * N, N:]
            q_re, q_im = probe[m, 0], probe[m, 1]
            o_re += q_re * g_re + q_im * g_im
            o_im += q_re * g_im - q_im * g_re
            probe_grad[m, 0] += p_re * g_re + p_im * g_im
            probe_grad[m, 1] += p_re * g_im - p_im * g_re
        for part, value in ((0, o_re), (1, o_im)):
            x = pltpu.roll(value.reshape(groups, 8, N), shift, 2)
            x = pltpu.roll(x, down_by, 1)
            blank = jnp.zeros((1, 8, N), F32)
            x = jnp.where(step >= down_by, jnp.concatenate([x, blank]), jnp.concatenate([blank, x]))
            grad[part, pl.ds(group, groups + 1), :, pl.ds(first, N)] += jnp.where(kept, x, 0.0)
            grad[part, pl.ds(group, groups + 1), :, pl.ds(second, N)] += jnp.where(kept, 0.0, x)
        return carry

    lax.fori_loop(0, slots, one_slot, 0)

    def block(start, count, lane, width):
        return grad[:, start // 8:(start + count) // 8, :, lane:lane + width].reshape(2, count, width)

    center[...] = block(HALF, size, N, size)
    up[...] = block(0, HALF, N, size)
    down[...] = block(low_edge, HALF, N, size)
    pack_l[...] = pack_high(block(HALF, size, 0, N))
    pack_r[...] = pack_low(block(HALF, size, high_edge, N))
    k0[...] = pack_high(block(0, HALF, 0, N))
    k1[...] = pack_low(block(0, HALF, high_edge, N))
    k2[...] = pack_high(block(low_edge, HALF, 0, N))
    k3[...] = pack_low(block(low_edge, HALF, high_edge, N))


def compute(rows, cols, pos, count, obj, halos, probe, measured):
    size = obj.shape[1]
    grouped = lambda x: x.reshape(2, -1, 8, x.shape[-1])
    obj, halos = grouped(obj), [grouped(x) for x in halos[:2]] + list(halos[2:])
    shape = lambda *dims: jax.ShapeDtypeStruct(dims, F32)
    return pl.pallas_call(
        functools.partial(compute_kernel, rows, cols),
        out_shape=[shape(2, size, size)] + [shape(2, HALF, size)] * 2 + [shape(2, size // 2, N)] * 2
        + [shape(2, HALF // 2, N)] * 4 + [shape(*probe.shape)],
        in_specs=[SMEM, SMEM] + [ANY] * 9 + [VMEM] * 3,
        out_specs=[VMEM] * 10,
        scratch_shapes=[
            pltpu.VMEM((2, (size + N) // 8, 8, size + 2 * N), F32),
            pltpu.VMEM((2, (size + N) // 8, 8, size + 2 * N), F32),
            pltpu.VMEM((2, 2, size // 2, N), F32),
            pltpu.VMEM((4, 2, HALF // 2, N), F32),
            pltpu.SemaphoreType.DMA((9,)),
        ],
        compiler_params=pltpu.CompilerParams(vmem_limit_bytes=48 * 1024 * 1024),
        name="slots",
    )(pos, count, obj, *halos, probe, measured, jnp.asarray(tables()))


def peers():
    r, c = lax.axis_index("row"), lax.axis_index("col")
    y, z_hi = r // 4, r % 4
    x, z_lo, core = c // 4, c // 2 % 2, c % 2
    along_x = [(r, (x + k) % 4 * 4 + c % 4) for k in (1, 2, 3)]
    along_y = [((y + k) % 4 * 4 + z_hi, c) for k in (1, 2, 3)]
    z = z_hi * 2 + z_lo
    along_z = []
    for k in range(1, 8):
        other = (z + k) % 8
        along_z.append((y * 4 + other // 2, x * 4 + other % 2 * 2 + core))
    return x, y, z, core, along_x, along_y, along_z, (r, c + 1 - 2 * core)


def remote(src, dst, send_sem, recv_sem, device):
    return pltpu.make_async_remote_copy(
        src_ref=src, dst_ref=dst, send_sem=send_sem, recv_sem=recv_sem, device_id=device, device_id_type=MESH)


def sum_everywhere(total, full, from_core, in_a, in_b, in_c, in_d, in_z, send_sem, recv_sem, scale):
    x, y, z, core, along_x, along_y, along_z, sibling = peers()
    rows = total.shape[0]
    half, quarter = rows // 2, rows // 4
    piece, small = quarter // 4, quarter // 16
    mine = core * half
    used = [0]

    def send(src, dst, device):
        i = used[0]
        used[0] += 1
        copy = remote(src, dst, send_sem.at[i], recv_sem.at[i], device)
        copy.start()
        return copy

    def finish(copies):
        for copy in copies:
            copy.wait()

    at = lambda ref, start, count: ref.at[pl.ds(pl.multiple_of(start, 8), count), :]
    span = lambda start, count: pl.ds(pl.multiple_of(start, 8), count)
    finish([send(at(total, half - mine, half), from_core, sibling)])
    total[span(mine, half), :] += from_core[...]
    a, b = mine, mine + quarter
    copies = [send(at(total, a + (x + k) % 4 * piece, piece), in_a.at[k - 1], along_x[k - 1]) for k in (1, 2, 3)]
    copies += [send(at(total, b + (y + k) % 4 * piece, piece), in_b.at[k - 1], along_y[k - 1]) for k in (1, 2, 3)]
    finish(copies)
    a, b = a + x * piece, b + y * piece
    total[span(a, piece), :] += in_a[0] + in_a[1] + in_a[2]
    total[span(b, piece), :] += in_b[0] + in_b[1] + in_b[2]
    copies = [send(at(total, a + (y + k) % 4 * small, small), in_c.at[k - 1], along_y[k - 1]) for k in (1, 2, 3)]
    copies += [send(at(total, b + (x + k) % 4 * small, small), in_d.at[k - 1], along_x[k - 1]) for k in (1, 2, 3)]
    finish(copies)
    a_own, b_own = a + y * small, b + x * small
    in_z[z, :small] = total[span(a_own, small), :] + (in_c[0] + in_c[1] + in_c[2])
    in_z[z, small:] = total[span(b_own, small), :] + (in_d[0] + in_d[1] + in_d[2])
    finish([send(in_z.at[z], in_z.at[z], along_z[k - 1]) for k in range(1, 8)])
    summed = in_z[0]
    for k in range(1, 8):
        summed = summed + in_z[k]
    summed = summed * scale
    full[span(a_own, small), :] = summed[:small]
    full[span(b_own, small), :] = summed[small:]
    copies = [send(at(full, a_own, small), at(full, a_own, small), device) for device in along_y]
    copies += [send(at(full, b_own, small), at(full, b_own, small), device) for device in along_x]
    finish(copies)
    copies = [send(at(full, a, piece), at(full, a, piece), device) for device in along_x]
    copies += [send(at(full, b, piece), at(full, b, piece), device) for device in along_y]
    finish(copies)
    finish([send(at(full, mine, half), at(full, mine, half), sibling)])


def return_kernel(rows, cols, scale, center, *refs):
    rims, probe_part = refs[:8], refs[8]
    out, full = refs[9:11]
    landing, total = refs[11:19], refs[19]
    scratch = refs[20:26]
    rim_send, rim_recv, send_sem, recv_sem, load_sem = refs[26:]
    near = neighbours(rows, cols)
    load = pltpu.make_async_copy(probe_part, total, load_sem)
    load.start()
    barrier = pltpu.get_barrier_semaphore()
    x, y, z, core, along_x, along_y, along_z, sibling = peers()
    others = along_x + along_y + along_z + [sibling]
    for device in others:
        pl.semaphore_signal(barrier, inc=1, device_id=device, device_id_type=MESH)
    for there, device in near:
        @pl.when(there)
        def _():
            pl.semaphore_signal(barrier, inc=1, device_id=device, device_id_type=MESH)
    beside = sum(there.astype(jnp.int32) for there, _ in near)
    pl.semaphore_wait(barrier, len(others) + beside)
    copies = [remote(rims[side], landing[OPPOSITE[side]], rim_send.at[side], rim_recv.at[OPPOSITE[side]],
                     near[side][1]) for side in range(8)]
    for side in range(8):
        @pl.when(near[side][0])
        def _():
            copies[side].start()
    load.wait()
    sum_everywhere(total, full, *scratch, send_sem, recv_sem, scale)
    out[...] = center[...]
    size = out.shape[1]

    def add(packed, row, is_low):
        k = packed.shape[1]
        lane = lax.broadcasted_iota(jnp.int32, (2, k, N), 2)
        turned = pltpu.roll(packed, HALF, 2)
        first, second = (packed, turned) if is_low else (turned, packed)
        kept = (lane < HALF) if is_low else (lane >= HALF)
        at = 0 if is_low else size - N
        out[:, row:row + k, at:at + N] += jnp.where(kept, first, 0.0)
        out[:, row + k:row + 2 * k, at:at + N] += jnp.where(kept, second, 0.0)

    for side in range(8):
        @pl.when(near[side][0])
        def _():
            copies[side].wait_send()
            copies[OPPOSITE[side]].wait_recv()
            if side == 0:
                out[:, :HALF, :] += landing[0][...]
            elif side == 1:
                out[:, size - HALF:, :] += landing[1][...]
            elif side < 4:
                add(landing[side][...], 0, side == 2)
            else:
                add(landing[side][...], 0 if side < 6 else size - HALF, side in (4, 6))


def return_rims(rows, cols, scale, center, rims, probe_part):
    size = center.shape[1]
    total = probe_part.reshape(-1, N)
    height = total.shape[0]
    vm = lambda *dims: pltpu.VMEM(dims, F32)
    quarter = height // 4
    out, full = pl.pallas_call(
        functools.partial(return_kernel, rows, cols, scale),
        out_shape=[jax.ShapeDtypeStruct(center.shape, F32), jax.ShapeDtypeStruct(total.shape, F32)],
        in_specs=[VMEM] + [ANY] * 9,
        out_specs=[VMEM] * 2,
        scratch_shapes=[vm(*x.shape) for x in rims] + [
            vm(height, N), vm(height // 2, N),
            vm(3, quarter // 4, N), vm(3, quarter // 4, N), vm(3, quarter // 16, N), vm(3, quarter // 16, N),
            vm(8, quarter // 8, N),
            pltpu.SemaphoreType.DMA((8,)), pltpu.SemaphoreType.DMA((8,)),
            pltpu.SemaphoreType.DMA((33,)), pltpu.SemaphoreType.DMA((33,)), pltpu.SemaphoreType.DMA,
        ],
        compiler_params=pltpu.CompilerParams(
            collective_id=1, has_side_effects=True, vmem_limit_bytes=32 * 1024 * 1024),
        name="rims",
    )(center, *rims, total)
    return out, full.reshape(probe_part.shape)


def local(rows, cols, object_field, probe, positions, counts, measured):
    halos = exchange_halo(object_field, rows, cols)
    center, *rims, probe_part = compute(
        rows, cols, positions, counts, object_field, halos, probe, measured[0, 0])
    scale = 1.0 / math.sqrt(rows * cols * measured.shape[2])
    return return_rims(rows, cols, scale, center, rims, probe_part)


def solution(mesh):
    placed = (
        P(None, "row", "col"),
        P(),
        P("row", "col", None, None),
        P("row", "col"),
        P("row", "col", None, None, None),
    )
    return jax.shard_map(
        functools.partial(local, mesh.shape["row"], mesh.shape["col"]),
        mesh=mesh, in_specs=placed, out_specs=(P(None, "row", "col"), P()), check_vma=False)
```

```python
import functools
import math

import jax
import jax.numpy as jnp
import numpy as np
from jax import lax
from jax.experimental import pallas as pl
from jax.experimental.pallas import tpu as pltpu
from jax.sharding import PartitionSpec as P

MESH = pl.DeviceIdType.MESH
UNROLL = 4
VLIM = 60
PIECES = 8
RELEASE = (1, 1, 1, 1, 2, 1)
ANY = pl.BlockSpec(memory_space=pl.ANY)
VMEM = pl.BlockSpec(memory_space=pltpu.VMEM)
INSPEC = ANY
SMEM = pl.BlockSpec(memory_space=pltpu.SMEM)
F32 = jnp.float32
BF16 = jnp.bfloat16
N = 128
HALF = 64
SIDES = ((-1, 0), (1, 0), (0, -1), (0, 1), (-1, -1), (-1, 1), (1, -1), (1, 1))
OPPOSITE = tuple(SIDES.index((-a, -b)) for a, b in SIDES)


def neighbours(rows, cols):
    r, c = lax.axis_index("row"), lax.axis_index("col")
    out = []
    for dr, dc in SIDES:
        there = True
        if dr:
            there = (r > 0) if dr < 0 else (r < rows - 1)
        if dc:
            col_there = (c > 0) if dc < 0 else (c < cols - 1)
            there = col_there if there is True else jnp.logical_and(there, col_there)
        out.append((there, (r + dr, c + dc)))
    return out


def pack_low(tile):
    k = tile.shape[1] // 2
    lane = lax.broadcasted_iota(jnp.int32, (2, k, N), 2)
    return jnp.where(lane < HALF, tile[:, :k], pltpu.roll(tile[:, k:], HALF, 2))


def pack_high(tile):
    k = tile.shape[1] // 2
    lane = lax.broadcasted_iota(jnp.int32, (2, k, N), 2)
    return jnp.where(lane < HALF, pltpu.roll(tile[:, :k], HALF, 2), tile[:, k:])


def tables():
    ramp = np.arange(N)
    angles = 2.0 * math.pi / N * (ramp[:, None] * ramp[None, :] % N)
    cos, sin = np.cos(angles) / math.sqrt(N), np.sin(angles) / math.sqrt(N)
    minus = np.block([[cos, -sin], [sin, cos]]).astype(np.float32)
    return np.stack([minus, minus.T])


def each(count, body, unroll):
    def some(i, carry):
        for k in range(unroll):
            body(i * unroll + k)
        return carry

    lax.fori_loop(0, count // unroll, some, 0)


def split(x):
    high = x.astype(BF16)
    return high, (x - high.astype(F32)).astype(BF16)


def dot(a, b):
    return jnp.dot(a, b, preferred_element_type=F32)


def times_table(x, high, low):
    x_high, x_low = split(x)
    return dot(x_high, high) + (dot(x_low, high) + dot(x_high, low))


def table_times(high, low, x):
    x_high, x_low = split(x)
    return dot(high, x_high) + (dot(high, x_low) + dot(low, x_high))


def peers():
    r, c = lax.axis_index("row"), lax.axis_index("col")
    y, z_hi = r // 4, r % 4
    x, z_lo, core = c // 4, c // 2 % 2, c % 2
    plane = [((y + k // 4) % 4 * 4 + z_hi, (x + k % 4) % 4 * 4 + c % 4) for k in range(1, 16)]
    z = z_hi * 2 + z_lo
    along_z = []
    for k in range(1, 8):
        other = (z + k) % 8
        along_z.append((y * 4 + other // 2, x * 4 + other % 2 * 2 + core))
    return x, y, z, core, plane, along_z, (r, c + 1 - 2 * core)


def remote(src, dst, send_sem, recv_sem, device):
    return pltpu.make_async_remote_copy(
        src_ref=src, dst_ref=dst, send_sem=send_sem, recv_sem=recv_sem, device_id=device, device_id_type=MESH)


def sum_everywhere(ring, total, full, from_core, in_xy, in_z, send_sem, recv_sem, scale):
    x, y, z, core, plane, along_z, sibling = ring
    rows = total.shape[0]
    half, piece = rows // 2, rows // 32
    mine = core * half
    own = mine + (y * 4 + x) * piece
    used = [0]

    def send(src, dst, device):
        i = used[0]
        used[0] += 1
        copy = remote(src, dst, send_sem.at[i], recv_sem.at[i], device)
        copy.start()
        return copy

    def finish(copies):
        for copy in copies:
            copy.wait()

    span = lambda start, count: pl.ds(pl.multiple_of(start, 8), count)
    at = lambda ref, start, count: ref.at[span(start, count), :]

    def steps():
        copies = [send(at(total, half - mine, half), from_core, sibling)]
        yield
        finish(copies)
        total[span(mine, half), :] += from_core[...]
        copies = [send(at(total, mine + ((y + k // 4) % 4 * 4 + (x + k % 4) % 4) * piece, piece), in_xy.at[k - 1],
                       plane[k - 1]) for k in range(1, 16)]
        yield
        finish(copies)
        in_z[z] = total[span(own, piece), :] + sum(in_xy[k] for k in range(15))
        copies = [send(in_z.at[z], in_z.at[z], device) for device in along_z]
        yield
        finish(copies)
        full[span(own, piece), :] = sum(in_z[k] for k in range(8)) * scale
        copies = [send(at(full, own, piece), at(full, own, piece), device) for device in plane]
        yield
        finish(copies)
        copies = [send(at(full, mine, half), at(full, mine, half), sibling)]
        yield
        finish(copies)
        yield

    run = steps()
    return lambda: next(run)


def spread(x, k):
    return x, pltpu.roll(x, HALF, 2)


def turn_lanes(x, by):
    lane = lax.broadcasted_iota(jnp.int32, (8 * x.shape[0], N), 1)
    return jnp.take_along_axis(x.reshape(-1, N), (lane + (N - by)) & (N - 1), axis=1).reshape(x.shape)


def turn_rows(x, by):
    index = (lax.broadcasted_iota(jnp.int32, (8, N), 0) + (8 - by)) & 7
    return jnp.stack([jnp.take_along_axis(x[k], index, axis=0) for k in range(x.shape[0])])


def kernel(rows, cols, scale, pos_in, count_in, obj, probe_in, measured_in, table_in, out, full,
           pos, count, ext, field, probe, measured, table_whole, table, patches, mids, sums, strips, strips_in, corners, corners_in,
           moved, rim_sides, rim_corners, land_up, land_down, land_sides, land_corners,
           total, from_core, in_xy, in_z, load_sem, halo_send, halo_recv, rim_send, rim_recv, send_sem, recv_sem):
    modes, slots = probe.shape[0], measured.shape[0]
    size = out.shape[1]
    tiles = size // N + 2
    edge, far_edge = HALF // 8, (HALF + size) // 8
    groups = N // 8
    near = neighbours(rows, cols)

    loads = [pltpu.make_async_copy(a, b, load_sem.at[i]) for i, (a, b) in enumerate((
        (obj, ext.at[:, pl.ds(edge, size // 8), :, pl.ds(N, size)]),
        (pos_in, pos), (count_in, count), (probe_in, probe), (measured_in, measured), (table_in, table_whole)))]
    for load in loads:
        load.start()

    barrier = pltpu.get_barrier_semaphore()
    ring = peers()
    others = ring[-3] + ring[-2] + [ring[-1]]
    for device in others:
        pl.semaphore_signal(barrier, inc=1, device_id=device, device_id_type=MESH)
    for there, device in near:
        @pl.when(there)
        def _():
            pl.semaphore_signal(barrier, inc=1, device_id=device, device_id_type=MESH)
    pl.semaphore_wait(barrier, len(others) + sum(there.astype(jnp.int32) for there, _ in near))

    sources = [obj.at[:, pl.ds(0, edge)], obj.at[:, pl.ds(size // 8 - edge, edge)],
               strips.at[0], strips.at[1]] + [corners.at[i] for i in range(4)]
    landing = [ext.at[:, pl.ds(0, edge), :, pl.ds(N, size)], ext.at[:, pl.ds(far_edge, edge), :, pl.ds(N, size)],
               strips_in.at[0], strips_in.at[1]] + [corners_in.at[i] for i in range(4)]
    halo = [remote(sources[i], landing[OPPOSITE[i]], halo_send.at[i], halo_recv.at[OPPOSITE[i]], near[i][1])
            for i in range(8)]

    def start(copies, side):
        @pl.when(near[side][0])
        def _():
            copies[side].start()

    start(halo, 0)
    start(halo, 1)
    loads[0].wait()
    first_tile = ext[:, edge:far_edge, :, N:2 * N].reshape(2, size, N)
    last_tile = ext[:, edge:far_edge, :, size:size + N].reshape(2, size, N)
    strips[0] = pack_low(first_tile)
    start(halo, 2)
    strips[1] = pack_high(last_tile)
    start(halo, 3)
    corners[0] = pack_low(first_tile[:, :HALF])
    corners[1] = pack_high(last_tile[:, :HALF])
    corners[2] = pack_low(first_tile[:, size - HALF:])
    corners[3] = pack_high(last_tile[:, size - HALF:])
    for side in range(4, 8):
        start(halo, side)
    total[...] = jnp.zeros_like(total)
    for g in (0, groups + 2):
        moved[:, :, g] = jnp.zeros((slots, 2, 8, size + 2 * N), F32)
    for load in loads[1:]:
        load.wait()
    table[0], table[1] = split(table_whole[0])
    table[2], table[3] = split(table_whole[1])
    for side in range(8):
        @pl.when(jnp.logical_not(near[side][0]))
        def _():
            landing[side][...] = jnp.zeros(landing[side].shape, F32)
    for t in range(1, tiles - 1):
        field[:, t, edge:far_edge] = ext[:, edge:far_edge, :, t * N:(t + 1) * N]
    for side in range(8):
        @pl.when(near[side][0])
        def _():
            halo[side].wait_send()
            halo[OPPOSITE[side]].wait_recv()

    def unpack(packed, at, lane, is_low):
        k = packed.shape[1] // 8
        as_is, turned = spread(packed, k)
        first, second = (as_is, turned) if is_low else (turned, as_is)
        field[:, lane // N, at:at + k] = first.reshape(2, k, 8, N)
        field[:, lane // N, at + k:at + 2 * k] = second.reshape(2, k, 8, N)

    unpack(strips_in[0], edge, 0, False)
    unpack(strips_in[1], edge, N + size, True)
    unpack(corners_in[0], 0, 0, False)
    unpack(corners_in[1], 0, N + size, True)
    unpack(corners_in[2], far_edge, 0, False)
    unpack(corners_in[3], far_edge, N + size, True)

    for t in range(1, tiles - 1):
        field[:, t, :edge] = ext[:, :edge, :, t * N:(t + 1) * N]
        field[:, t, far_edge:] = ext[:, far_edge:, :, t * N:(t + 1) * N]

    minus_high, minus_low, plus_high, plus_low = (table[i] for i in range(4))
    lane = lax.broadcasted_iota(jnp.int32, (groups + 1, 8, N), 2)
    step = lax.broadcasted_iota(jnp.int32, (groups + 1, 8, N), 1)
    live = count[0, 0]

    def place(slot):
        row, col = pos[0, slot], pos[1, slot] + HALF
        return row // 8, row % 8, col // N, col % N

    def one_slot(slot):
        group, down_by, tile, shift = place(slot)
        kept = lane >= shift

        def cut(part):
            a, b = (jnp.stack([field[part, tile + t, group + k] for k in range(groups + 1)]) for t in (0, 1))
            x = turn_lanes(jnp.where(kept, a, b), N - shift)
            x = turn_rows(x, 8 - down_by)
            return jnp.where(step[:groups] < 8 - down_by, x[:groups], x[1:]).reshape(N, N)

        p_re, p_im = cut(0), cut(1)
        patches[slot, 0] = p_re
        patches[slot, 1] = p_im
        waves = []
        for m in range(modes):
            q_re, q_im = probe[m, 0], probe[m, 1]
            waves.append(jnp.concatenate([q_re * p_re - q_im * p_im, q_re * p_im + q_im * p_re], axis=1))
        half = times_table(jnp.concatenate(waves, axis=0), minus_high, minus_low)
        half = jnp.concatenate(
            [jnp.concatenate([half[m * N:(m + 1) * N, :N], half[m * N:(m + 1) * N, N:]], axis=0)
             for m in range(modes)], axis=1)
        far = table_times(plus_high, plus_low, half)
        power = far[:N] * far[:N] + far[N:] * far[N:]
        intensity = sum(power[:, m * N:(m + 1) * N] for m in range(modes))
        alive = jnp.where(slot < live, 1.0, 0.0).astype(F32)
        factor = (1.0 - measured[slot] * lax.rsqrt(intensity + 0.1)) * alive
        wide = jnp.concatenate([factor] * modes, axis=1)
        far = far * jnp.concatenate([wide, wide], axis=0)
        half = table_times(minus_high, minus_low, far)
        for m in range(modes):
            mids[slot, m, :, :N] = half[:N, m * N:(m + 1) * N]
            mids[slot, m, :, N:] = half[N:, m * N:(m + 1) * N]

    each(slots, one_slot, UNROLL)

    def last_step(slot, some):
        g = times_table(mids[slot, some[0]:some[-1] + 1].reshape(-1, 2 * N), plus_high, plus_low)
        p_re, p_im = patches[slot, 0], patches[slot, 1]
        o_re = jnp.zeros((N, N), F32)
        o_im = jnp.zeros((N, N), F32)
        for k, m in enumerate(some):
            g_re, g_im = g[k * N:(k + 1) * N, :N], g[k * N:(k + 1) * N, N:]
            q_re, q_im = probe[m, 0], probe[m, 1]
            o_re += q_re * g_re + q_im * g_im
            o_im += q_re * g_im - q_im * g_re
            total[2 * m * N:(2 * m + 1) * N] += p_re * g_re + p_im * g_im
            total[(2 * m + 1) * N:(2 * m + 2) * N] += p_re * g_im - p_im * g_re
        return o_re, o_im

    def first_modes(slot):
        sums[slot, 0], sums[slot, 1] = last_step(slot, early)

    def last_modes(slot):
        _, down_by, tile, shift = place(slot)
        o_re, o_im = last_step(slot, late)
        blank = jnp.zeros((1, 8, N), F32)
        for part, value in ((0, sums[slot, 0] + o_re), (1, sums[slot, 1] + o_im)):
            x = turn_lanes(value.reshape(groups, 8, N), shift)
            x = turn_rows(x, down_by)
            x = jnp.where(step >= down_by, jnp.concatenate([x, blank]), jnp.concatenate([blank, x]))
            for t in range(tiles):
                from_start = lane[:1] + (t * N - shift) - tile * N
                inside = jnp.logical_and(from_start >= 0, from_start < N)
                moved[slot, part, 1:groups + 2, :, t * N:(t + 1) * N] = jnp.where(inside, x, 0.0)

    early, late = tuple(range(modes // 2)), tuple(range(modes // 2, modes))
    cut_at = 2 * len(early) * N
    advance_a, advance_b = (
        sum_everywhere(ring, total.at[rows_of], full.at[rows_of], from_core.at[i], in_xy.at[i], in_z.at[i],
                       send_sem.at[i], recv_sem.at[i], scale)
        for i, rows_of in enumerate((pl.ds(0, cut_at), pl.ds(cut_at, total.shape[0] - cut_at))))
    each(slots, first_modes, UNROLL)
    advance_a()
    each(slots, last_modes, UNROLL)
    advance_a()
    advance_b()
    starts = [place(slot)[0] for slot in range(slots)]

    def gather(g):
        at = [jnp.clip(g - start + 1, 0, groups + 2) for start in starts]
        for part in (0, 1):
            ext[part, g] = sum(moved[slot, part, at[slot]] for slot in range(slots))

    each(ext.shape[1], gather, 1)
    advance_b()
    block = lambda at, k, lane: ext[:, at:at + k, :, lane:lane + N].reshape(2, 8 * k, N)
    rim_sides[0] = pack_high(block(edge, size // 8, 0))
    rim_sides[1] = pack_low(block(edge, size // 8, N + size))
    rim_corners[0] = pack_high(block(0, edge, 0))
    rim_corners[1] = pack_low(block(0, edge, N + size))
    rim_corners[2] = pack_high(block(far_edge, edge, 0))
    rim_corners[3] = pack_low(block(far_edge, edge, N + size))

    per_row, per_side = edge // PIECES, size // 2 // PIECES
    rims = []
    for p in range(PIECES):
        rows_of, part_of = pl.ds(p * per_row, per_row), pl.ds(p * per_side, per_side)
        rims.append([
            (0, ext.at[:, rows_of, :, pl.ds(N, size)], land_down.at[:, rows_of]),
            (1, ext.at[:, pl.ds(far_edge + p * per_row, per_row), :, pl.ds(N, size)], land_up.at[:, rows_of]),
            (2, rim_sides.at[0, :, part_of], land_sides.at[1, :, part_of]),
            (3, rim_sides.at[1, :, part_of], land_sides.at[0, :, part_of])])
    for i in range(4):
        rims[i * PIECES // 4].append((4 + i, rim_corners.at[i], land_corners.at[OPPOSITE[4 + i] - 4]))
    rims = [[(side, remote(src, dst, rim_send.at[p, side], rim_recv.at[p, OPPOSITE[side]], near[side][1]))
             for side, src, dst in piece] for p, piece in enumerate(rims)]
    left = list(rims)

    def release(count):
        for _ in range(min(count, len(left))):
            for side, copy in left.pop(0):
                @pl.when(near[side][0])
                def _():
                    copy.start()

    release(RELEASE[0])
    advance_a()
    release(RELEASE[1])
    out[...] = ext[:, edge:far_edge, :, N:N + size].reshape(2, size, size)
    advance_b()
    release(RELEASE[2])
    advance_a()
    release(RELEASE[3])
    advance_b()
    release(RELEASE[4])
    advance_a()
    release(RELEASE[5])
    advance_b()
    release(PIECES)
    advance_a()
    advance_b()

    def add(packed, row, is_low):
        k = packed.shape[1]
        lane_of = lax.broadcasted_iota(jnp.int32, (2, k, N), 2)
        as_is, turned = spread(packed, k)
        first, second = (as_is, turned) if is_low else (turned, as_is)
        inside = (lane_of < HALF) if is_low else (lane_of >= HALF)
        at = 0 if is_low else size - N
        out[:, row:row + k, at:at + N] += jnp.where(inside, first, 0.0)
        out[:, row + k:row + 2 * k, at:at + N] += jnp.where(inside, second, 0.0)

    for piece in rims:
        for side, copy in piece:
            @pl.when(near[side][0])
            def _():
                copy.wait_send()

            @pl.when(near[OPPOSITE[side]][0])
            def _():
                copy.wait_recv()

    for side in range(8):
        @pl.when(near[side][0])
        def _():
            if side == 0:
                out[:, :HALF, :] += land_up[...].reshape(2, HALF, size)
            elif side == 1:
                out[:, size - HALF:, :] += land_down[...].reshape(2, HALF, size)
            elif side < 4:
                add(land_sides[side - 2], 0, side == 2)
            else:
                add(land_corners[side - 4], 0 if side < 6 else size - HALF, side in (4, 6))


def local(rows, cols, object_field, probe, positions, counts, measured):
    size = object_field.shape[1]
    slots, modes = measured.shape[2], probe.shape[0]
    scale = 1.0 / math.sqrt(rows * cols * slots)
    height = 2 * modes * N
    vm = lambda *dims: pltpu.VMEM(dims, F32)
    dma = lambda *count: pltpu.SemaphoreType.DMA(count)
    strip, side, corner = (2, HALF // 8, 8, size), (2, 2, size // 2, N), (4, 2, HALF // 2, N)
    out, full = pl.pallas_call(
        functools.partial(kernel, rows, cols, scale),
        out_shape=[jax.ShapeDtypeStruct(object_field.shape, F32), jax.ShapeDtypeStruct((height, N), F32)],
        in_specs=[INSPEC] * 6,
        out_specs=[VMEM] * 2,
        scratch_shapes=[
            pltpu.SMEM((2, slots), jnp.int32), pltpu.SMEM(counts.shape, jnp.int32),
            vm(2, (size + N) // 8, 8, size + 2 * N), vm(2, size // N + 2, (size + N) // 8, 8, N), vm(*probe.shape), vm(slots, N, N),
            vm(2, 2 * N, 2 * N), pltpu.VMEM((4, 2 * N, 2 * N), BF16),
            vm(slots, 2, N, N), vm(slots, modes, N, 2 * N), vm(slots, 2, N, N),
            vm(*side), vm(*side), vm(*corner), vm(*corner),
            vm(slots, 2, N // 8 + 3, 8, size + 2 * N),
            vm(*side), vm(*corner),
            vm(*strip), vm(*strip), vm(*side), vm(*corner),
            vm(height, N), vm(2, height // 4, N), vm(2, 15, height // 64, N), vm(2, 8, height // 64, N),
            dma(6), dma(8), dma(8), dma(PIECES, 8), dma(PIECES, 8), dma(2, 39), dma(2, 39),
        ],
        compiler_params=pltpu.CompilerParams(
            collective_id=0, has_side_effects=True, vmem_limit_bytes=VLIM * 1024 * 1024),
        name="step",
    )(positions[0, 0].T, counts, object_field.reshape(2, size // 8, 8, size), probe, measured[0, 0], jnp.asarray(tables()))
    return out, full.reshape(probe.shape)


def solution(mesh):
    placed = (
        P(None, "row", "col"),
        P(),
        P("row", "col", None, None),
        P("row", "col"),
        P("row", "col", None, None, None),
    )
    return jax.shard_map(
        functools.partial(local, mesh.shape["row"], mesh.shape["col"]),
        mesh=mesh, in_specs=placed, out_specs=(P(None, "row", "col"), P()), check_vma=False)
```

```python
import functools
import math

import jax
import jax.numpy as jnp
import numpy as np
from jax import lax
from jax.experimental import pallas as pl
from jax.experimental.pallas import tpu as pltpu
from jax.sharding import PartitionSpec as P

MESH = pl.DeviceIdType.MESH
UNROLL = 4
VLIM = 60
PIECES = 8
SHARES = 4
RELEASE = (1, 1, 1, 1, 2, 1)
ANY = pl.BlockSpec(memory_space=pl.ANY)
VMEM = pl.BlockSpec(memory_space=pltpu.VMEM)
INSPEC = ANY
SMEM = pl.BlockSpec(memory_space=pltpu.SMEM)
F32 = jnp.float32
BF16 = jnp.bfloat16
N = 128
HALF = 64
SIDES = ((-1, 0), (1, 0), (0, -1), (0, 1), (-1, -1), (-1, 1), (1, -1), (1, 1))
OPPOSITE = tuple(SIDES.index((-a, -b)) for a, b in SIDES)


def neighbours(rows, cols):
    r, c = lax.axis_index("row"), lax.axis_index("col")
    out = []
    for dr, dc in SIDES:
        there = True
        if dr:
            there = (r > 0) if dr < 0 else (r < rows - 1)
        if dc:
            col_there = (c > 0) if dc < 0 else (c < cols - 1)
            there = col_there if there is True else jnp.logical_and(there, col_there)
        out.append((there, (r + dr, c + dc)))
    return out


def pack_low(tile):
    k = tile.shape[1] // 2
    lane = lax.broadcasted_iota(jnp.int32, (2, k, N), 2)
    return jnp.where(lane < HALF, tile[:, :k], pltpu.roll(tile[:, k:], HALF, 2))


def pack_high(tile):
    k = tile.shape[1] // 2
    lane = lax.broadcasted_iota(jnp.int32, (2, k, N), 2)
    return jnp.where(lane < HALF, pltpu.roll(tile[:, :k], HALF, 2), tile[:, k:])


def tables():
    ramp = np.arange(N)
    angles = 2.0 * math.pi / N * (ramp[:, None] * ramp[None, :] % N)
    cos, sin = np.cos(angles) / math.sqrt(N), np.sin(angles) / math.sqrt(N)
    minus = np.block([[cos, -sin], [sin, cos]]).astype(np.float32)
    return np.stack([minus, minus.T])


def each(count, body, unroll):
    def some(i, carry):
        body([i * unroll + k for k in range(unroll)])
        return carry

    lax.fori_loop(0, count // unroll, some, 0)


def split(x):
    high = x.astype(BF16)
    return high, (x - high.astype(F32)).astype(BF16)


def dot(a, b):
    return jnp.dot(a, b, preferred_element_type=F32)


def times_table(x, high, low):
    x_high, x_low = split(x)
    return dot(x_high, high) + (dot(x_low, high) + dot(x_high, low))


def table_times(high, low, x):
    x_high, x_low = split(x)
    both = dot(jnp.concatenate([high, low], axis=0), x_high)
    return both[:high.shape[0]] + (dot(high, x_low) + both[high.shape[0]:])


def peers():
    r, c = lax.axis_index("row"), lax.axis_index("col")
    y, z_hi = r // 4, r % 4
    x, z_lo, core = c // 4, c // 2 % 2, c % 2
    plane = [((y + k // 4) % 4 * 4 + z_hi, (x + k % 4) % 4 * 4 + c % 4) for k in range(1, 16)]
    z = z_hi * 2 + z_lo
    along_z = []
    for k in range(1, 8):
        other = (z + k) % 8
        along_z.append((y * 4 + other // 2, x * 4 + other % 2 * 2 + core))
    return x, y, z, core, plane, along_z, (r, c + 1 - 2 * core)


def remote(src, dst, send_sem, recv_sem, device):
    return pltpu.make_async_remote_copy(
        src_ref=src, dst_ref=dst, send_sem=send_sem, recv_sem=recv_sem, device_id=device, device_id_type=MESH)


def sum_everywhere(ring, total, full, from_core, in_xy, in_z, send_sem, recv_sem, scale):
    x, y, z, core, plane, along_z, sibling = ring
    rows = total.shape[0]
    half, piece = rows // 2, rows // 32
    mine = core * half
    own = mine + (y * 4 + x) * piece
    used = [0]

    def send(src, dst, device):
        i = used[0]
        used[0] += 1
        copy = remote(src, dst, send_sem.at[i], recv_sem.at[i], device)
        copy.start()
        return copy

    def finish(copies):
        for copy in copies:
            copy.wait()

    span = lambda start, count: pl.ds(pl.multiple_of(start, 8), count)
    at = lambda ref, start, count: ref.at[span(start, count), :]

    def steps():
        copies = [send(at(total, half - mine, half), from_core, sibling)]
        yield
        finish(copies)
        total[span(mine, half), :] += from_core[...]
        copies = [send(at(total, mine + ((y + k // 4) % 4 * 4 + (x + k % 4) % 4) * piece, piece), in_xy.at[k - 1],
                       plane[k - 1]) for k in range(1, 16)]
        yield
        finish(copies)
        in_z[z] = total[span(own, piece), :] + sum(in_xy[k] for k in range(15))
        copies = [send(in_z.at[z], in_z.at[z], device) for device in along_z]
        yield
        finish(copies)
        full[span(own, piece), :] = sum(in_z[k] for k in range(8)) * scale
        copies = [send(at(full, own, piece), at(full, own, piece), device) for device in plane]
        yield
        finish(copies)
        copies = [send(at(full, mine, half), at(full, mine, half), sibling)]
        yield
        finish(copies)
        yield

    run = steps()
    return lambda: next(run)


def spread(x, k):
    return x, pltpu.roll(x, HALF, 2)


def turn_lanes(x, by):
    lane = lax.broadcasted_iota(jnp.int32, (8 * x.shape[0], N), 1)
    return jnp.take_along_axis(x.reshape(-1, N), (lane + (N - by)) & (N - 1), axis=1).reshape(x.shape)


def turn_rows(x, by):
    index = (lax.broadcasted_iota(jnp.int32, (8, N), 0) + (8 - by)) & 7
    return jnp.stack([jnp.take_along_axis(x[k], index, axis=0) for k in range(x.shape[0])])


def kernel(rows, cols, scale, pos_in, count_in, obj, probe_in, measured_in, table_in, out, full,
           pos, count, ext, field, probe, measured, table_whole, table, patches, mids, sums, strips, strips_in, corners, corners_in,
           moved, rim_sides, rim_corners, land_up, land_down, land_sides, land_corners,
           total, from_core, in_xy, in_z, load_sem, halo_send, halo_recv, rim_send, rim_recv, send_sem, recv_sem):
    modes, slots = probe.shape[0], measured.shape[0]
    size = out.shape[1]
    tiles = size // N + 2
    edge, far_edge = HALF // 8, (HALF + size) // 8
    groups = N // 8
    near = neighbours(rows, cols)

    loads = [pltpu.make_async_copy(a, b, load_sem.at[i]) for i, (a, b) in enumerate((
        (obj, ext.at[:, pl.ds(edge, size // 8), :, pl.ds(N, size)]),
        (pos_in, pos), (count_in, count), (probe_in, probe), (measured_in, measured), (table_in, table_whole)))]
    for load in loads:
        load.start()

    barrier = pltpu.get_barrier_semaphore()
    ring = peers()
    others = ring[-3] + ring[-2] + [ring[-1]]
    for device in others:
        pl.semaphore_signal(barrier, inc=1, device_id=device, device_id_type=MESH)
    for there, device in near:
        @pl.when(there)
        def _():
            pl.semaphore_signal(barrier, inc=1, device_id=device, device_id_type=MESH)
    pl.semaphore_wait(barrier, len(others) + sum(there.astype(jnp.int32) for there, _ in near))

    sources = [obj.at[:, pl.ds(0, edge)], obj.at[:, pl.ds(size // 8 - edge, edge)],
               strips.at[0], strips.at[1]] + [corners.at[i] for i in range(4)]
    landing = [ext.at[:, pl.ds(0, edge), :, pl.ds(N, size)], ext.at[:, pl.ds(far_edge, edge), :, pl.ds(N, size)],
               strips_in.at[0], strips_in.at[1]] + [corners_in.at[i] for i in range(4)]
    halo = [remote(sources[i], landing[OPPOSITE[i]], halo_send.at[i], halo_recv.at[OPPOSITE[i]], near[i][1])
            for i in range(8)]

    def start(copies, side):
        @pl.when(near[side][0])
        def _():
            copies[side].start()

    start(halo, 0)
    start(halo, 1)
    loads[0].wait()
    first_tile = ext[:, edge:far_edge, :, N:2 * N].reshape(2, size, N)
    last_tile = ext[:, edge:far_edge, :, size:size + N].reshape(2, size, N)
    strips[0] = pack_low(first_tile)
    start(halo, 2)
    strips[1] = pack_high(last_tile)
    start(halo, 3)
    corners[0] = pack_low(first_tile[:, :HALF])
    corners[1] = pack_high(last_tile[:, :HALF])
    corners[2] = pack_low(first_tile[:, size - HALF:])
    corners[3] = pack_high(last_tile[:, size - HALF:])
    for side in range(4, 8):
        start(halo, side)
    total[...] = jnp.zeros_like(total)
    for g in (0, groups + 2):
        moved[:, :, g] = jnp.zeros((slots, 2, 8, size + 2 * N), F32)
    for load in loads[1:]:
        load.wait()
    table[0], table[1] = split(table_whole[0])
    table[2], table[3] = split(table_whole[1])
    for side in range(8):
        @pl.when(jnp.logical_not(near[side][0]))
        def _():
            landing[side][...] = jnp.zeros(landing[side].shape, F32)
    for t in range(1, tiles - 1):
        field[:, t, edge:far_edge] = ext[:, edge:far_edge, :, t * N:(t + 1) * N]
    for side in range(8):
        @pl.when(near[side][0])
        def _():
            halo[side].wait_send()
            halo[OPPOSITE[side]].wait_recv()

    def unpack(packed, at, lane, is_low):
        k = packed.shape[1] // 8
        as_is, turned = spread(packed, k)
        first, second = (as_is, turned) if is_low else (turned, as_is)
        field[:, lane // N, at:at + k] = first.reshape(2, k, 8, N)
        field[:, lane // N, at + k:at + 2 * k] = second.reshape(2, k, 8, N)

    unpack(strips_in[0], edge, 0, False)
    unpack(strips_in[1], edge, N + size, True)
    unpack(corners_in[0], 0, 0, False)
    unpack(corners_in[1], 0, N + size, True)
    unpack(corners_in[2], far_edge, 0, False)
    unpack(corners_in[3], far_edge, N + size, True)

    for t in range(1, tiles - 1):
        field[:, t, :edge] = ext[:, :edge, :, t * N:(t + 1) * N]
        field[:, t, far_edge:] = ext[:, far_edge:, :, t * N:(t + 1) * N]

    minus_high, minus_low, plus_high, plus_low = (table[i] for i in range(4))
    lane = lax.broadcasted_iota(jnp.int32, (groups + 1, 8, N), 2)
    step = lax.broadcasted_iota(jnp.int32, (groups + 1, 8, N), 1)
    live = count[0, 0]

    def place(slot):
        row, col = pos[0, slot], pos[1, slot] + HALF
        return row // 8, row % 8, col // N, col % N

    def waves_of(slot):
        group, down_by, tile, shift = place(slot)
        kept = lane >= shift

        def cut(part):
            a, b = (jnp.stack([field[part, tile + t, group + k] for k in range(groups + 1)]) for t in (0, 1))
            x = turn_lanes(jnp.where(kept, a, b), N - shift)
            x = turn_rows(x, 8 - down_by)
            return jnp.where(step[:groups] < 8 - down_by, x[:groups], x[1:]).reshape(N, N)

        p_re, p_im = cut(0), cut(1)
        patches[slot, 0] = p_re
        patches[slot, 1] = p_im
        waves = []
        for m in range(modes):
            q_re, q_im = probe[m, 0], probe[m, 1]
            waves.append(jnp.concatenate([q_re * p_re - q_im * p_im, q_re * p_im + q_im * p_re], axis=1))
        return waves

    def first_steps(some):
        half = times_table(jnp.concatenate(sum((waves_of(slot) for slot in some), []), axis=0), minus_high, minus_low)
        for k, slot in enumerate(some):
            along_rows(slot, half[k * modes * N:(k + 1) * modes * N])

    def along_rows(slot, half):
        half = jnp.concatenate(
            [jnp.concatenate([half[m * N:(m + 1) * N, :N], half[m * N:(m + 1) * N, N:]], axis=0)
             for m in range(modes)], axis=1)
        far = table_times(plus_high, plus_low, half)
        power = far[:N] * far[:N] + far[N:] * far[N:]
        intensity = sum(power[:, m * N:(m + 1) * N] for m in range(modes))
        alive = jnp.where(slot < live, 1.0, 0.0).astype(F32)
        factor = (1.0 - measured[slot] * lax.rsqrt(intensity + 0.1)) * alive
        wide = jnp.concatenate([factor] * modes, axis=1)
        far = far * jnp.concatenate([wide, wide], axis=0)
        half = table_times(minus_high, minus_low, far)
        for m in range(modes):
            mids[slot, m, :, :N] = half[:N, m * N:(m + 1) * N]
            mids[slot, m, :, N:] = half[N:, m * N:(m + 1) * N]

    each(slots, first_steps, UNROLL)

    def last_step(slots_now, some):
        height = len(some) * N
        x = [mids[slot, some[0]:some[-1] + 1].reshape(height, 2 * N) for slot in slots_now]
        g_all = times_table(jnp.concatenate(x, axis=0), plus_high, plus_low)
        result = []
        for i, slot in enumerate(slots_now):
            g = g_all[i * height:(i + 1) * height]
            p_re, p_im = patches[slot, 0], patches[slot, 1]
            o_re = jnp.zeros((N, N), F32)
            o_im = jnp.zeros((N, N), F32)
            for k, m in enumerate(some):
                g_re, g_im = g[k * N:(k + 1) * N, :N], g[k * N:(k + 1) * N, N:]
                q_re, q_im = probe[m, 0], probe[m, 1]
                o_re += q_re * g_re + q_im * g_im
                o_im += q_re * g_im - q_im * g_re
                total[2 * m * N:(2 * m + 1) * N] += p_re * g_re + p_im * g_im
                total[(2 * m + 1) * N:(2 * m + 2) * N] += p_re * g_im - p_im * g_re
            result.append((o_re, o_im))
        return result

    def first_modes(some):
        for slot, (o_re, o_im) in zip(some, last_step(some, early)):
            sums[slot, 0], sums[slot, 1] = o_re, o_im

    def last_modes(some):
        for slot, (o_re, o_im) in zip(some, last_step(some, late)):
            _, down_by, tile, shift = place(slot)
            blank = jnp.zeros((1, 8, N), F32)
            for part, value in ((0, sums[slot, 0] + o_re), (1, sums[slot, 1] + o_im)):
                x = turn_lanes(value.reshape(groups, 8, N), shift)
                x = turn_rows(x, down_by)
                x = jnp.where(step >= down_by, jnp.concatenate([x, blank]), jnp.concatenate([blank, x]))
                for t in range(tiles):
                    from_start = lane[:1] + (t * N - shift) - tile * N
                    inside = jnp.logical_and(from_start >= 0, from_start < N)
                    moved[slot, part, 1:groups + 2, :, t * N:(t + 1) * N] = jnp.where(inside, x, 0.0)

    early, late = tuple(range(modes // 2)), tuple(range(modes // 2, modes))
    cut_at = 2 * len(early) * N
    advance_a, advance_b = (
        sum_everywhere(ring, total.at[rows_of], full.at[rows_of], from_core.at[i], in_xy.at[i], in_z.at[i],
                       send_sem.at[i], recv_sem.at[i], scale)
        for i, rows_of in enumerate((pl.ds(0, cut_at), pl.ds(cut_at, total.shape[0] - cut_at))))
    each(slots, first_modes, UNROLL)
    advance_a()
    each(slots, last_modes, UNROLL)
    advance_a()
    advance_b()
    starts = [place(slot)[0] for slot in range(slots)]

    def gather(some):
        g, = some
        at = [jnp.clip(g - start + 1, 0, groups + 2) for start in starts]
        for part in (0, 1):
            ext[part, g] = sum(moved[slot, part, at[slot]] for slot in range(slots))

    each(ext.shape[1], gather, 1)
    advance_b()
    block = lambda at, k, lane: ext[:, at:at + k, :, lane:lane + N].reshape(2, 8 * k, N)
    rim_sides[0] = pack_high(block(edge, size // 8, 0))
    rim_sides[1] = pack_low(block(edge, size // 8, N + size))
    rim_corners[0] = pack_high(block(0, edge, 0))
    rim_corners[1] = pack_low(block(0, edge, N + size))
    rim_corners[2] = pack_high(block(far_edge, edge, 0))
    rim_corners[3] = pack_low(block(far_edge, edge, N + size))

    per_row, per_side = edge // PIECES, size // 2 // PIECES
    rims = []
    for p in range(PIECES):
        rows_of, part_of = pl.ds(p * per_row, per_row), pl.ds(p * per_side, per_side)
        rims.append([
            (0, ext.at[:, rows_of, :, pl.ds(N, size)], land_down.at[:, rows_of]),
            (1, ext.at[:, pl.ds(far_edge + p * per_row, per_row), :, pl.ds(N, size)], land_up.at[:, rows_of]),
            (2, rim_sides.at[0, :, part_of], land_sides.at[1, :, part_of]),
            (3, rim_sides.at[1, :, part_of], land_sides.at[0, :, part_of])])
    for i in range(4):
        rims[i * PIECES // 4].append((4 + i, rim_corners.at[i], land_corners.at[OPPOSITE[4 + i] - 4]))
    rims = [[(side, remote(src, dst, rim_send.at[p, side], rim_recv.at[p, OPPOSITE[side]], near[side][1]))
             for side, src, dst in piece] for p, piece in enumerate(rims)]
    left = list(rims)

    def release(count):
        for _ in range(min(count, len(left))):
            for side, copy in left.pop(0):
                @pl.when(near[side][0])
                def _():
                    copy.start()

    release(RELEASE[0])
    advance_a()
    release(RELEASE[1])
    out[...] = ext[:, edge:far_edge, :, N:N + size].reshape(2, size, size)
    advance_b()
    release(RELEASE[2])
    advance_a()
    release(RELEASE[3])
    advance_b()
    release(RELEASE[4])
    advance_a()
    release(RELEASE[5])
    advance_b()
    release(PIECES)
    advance_a()
    advance_b()

    def add(packed, row, is_low):
        k = packed.shape[1]
        lane_of = lax.broadcasted_iota(jnp.int32, (2, k, N), 2)
        as_is, turned = spread(packed, k)
        first, second = (as_is, turned) if is_low else (turned, as_is)
        inside = (lane_of < HALF) if is_low else (lane_of >= HALF)
        at = 0 if is_low else size - N
        out[:, row:row + k, at:at + N] += jnp.where(inside, first, 0.0)
        out[:, row + k:row + 2 * k, at:at + N] += jnp.where(inside, second, 0.0)

    for piece in rims:
        for side, copy in piece:
            @pl.when(near[side][0])
            def _():
                copy.wait_send()

            @pl.when(near[OPPOSITE[side]][0])
            def _():
                copy.wait_recv()

    for side in range(8):
        @pl.when(near[side][0])
        def _():
            if side == 0:
                out[:, :HALF, :] += land_up[...].reshape(2, HALF, size)
            elif side == 1:
                out[:, size - HALF:, :] += land_down[...].reshape(2, HALF, size)
            elif side < 4:
                add(land_sides[side - 2], 0, side == 2)
            else:
                add(land_corners[side - 4], 0 if side < 6 else size - HALF, side in (4, 6))


def hand_over_kernel(a, b, out_a, out_b, held_a, held_b, load_sem, store_sem):
    part_a, part_b = a.shape[1] // SHARES, b.shape[0] // SHARES
    loads, stores = [], []
    for i in range(SHARES):
        rows_a, rows_b = pl.ds(i * part_a, part_a), pl.ds(i * part_b, part_b)
        loads.append(pltpu.make_async_copy(a.at[:, rows_a], held_a.at[:, rows_a], load_sem.at[0, i]))
        loads.append(pltpu.make_async_copy(b.at[rows_b], held_b.at[rows_b], load_sem.at[1, i]))
        stores.append(pltpu.make_async_copy(held_a.at[:, rows_a], out_a.at[:, rows_a], store_sem.at[0, i]))
        stores.append(pltpu.make_async_copy(held_b.at[rows_b], out_b.at[rows_b], store_sem.at[1, i]))
    for load in loads:
        load.start()
    for load, store in zip(loads, stores):
        load.wait()
        store.start()
    for store in stores:
        store.wait()


def local(rows, cols, object_field, probe, positions, counts, measured):
    size = object_field.shape[1]
    slots, modes = measured.shape[2], probe.shape[0]
    scale = 1.0 / math.sqrt(rows * cols * slots)
    height = 2 * modes * N
    vm = lambda *dims: pltpu.VMEM(dims, F32)
    dma = lambda *count: pltpu.SemaphoreType.DMA(count)
    strip, side, corner = (2, HALF // 8, 8, size), (2, 2, size // 2, N), (4, 2, HALF // 2, N)
    out, full = pl.pallas_call(
        functools.partial(kernel, rows, cols, scale),
        out_shape=[jax.ShapeDtypeStruct(object_field.shape, F32), jax.ShapeDtypeStruct((height, N), F32)],
        in_specs=[INSPEC] * 6,
        out_specs=[VMEM] * 2,
        scratch_shapes=[
            pltpu.SMEM((2, slots), jnp.int32), pltpu.SMEM(counts.shape, jnp.int32),
            vm(2, (size + N) // 8, 8, size + 2 * N), vm(2, size // N + 2, (size + N) // 8, 8, N), vm(*probe.shape), vm(slots, N, N),
            vm(2, 2 * N, 2 * N), pltpu.VMEM((4, 2 * N, 2 * N), BF16),
            vm(slots, 2, N, N), vm(slots, modes, N, 2 * N), vm(slots, 2, N, N),
            vm(*side), vm(*side), vm(*corner), vm(*corner),
            vm(slots, 2, N // 8 + 3, 8, size + 2 * N),
            vm(*side), vm(*corner),
            vm(*strip), vm(*strip), vm(*side), vm(*corner),
            vm(height, N), vm(2, height // 4, N), vm(2, 15, height // 64, N), vm(2, 8, height // 64, N),
            dma(6), dma(8), dma(8), dma(PIECES, 8), dma(PIECES, 8), dma(2, 39), dma(2, 39),
        ],
        compiler_params=pltpu.CompilerParams(
            collective_id=0, has_side_effects=True, vmem_limit_bytes=VLIM * 1024 * 1024),
        name="step",
    )(positions[0, 0].T, counts, object_field.reshape(2, size // 8, 8, size), probe, measured[0, 0], jnp.asarray(tables()))
    out, full = pl.pallas_call(
        hand_over_kernel,
        out_shape=[jax.ShapeDtypeStruct(out.shape, F32), jax.ShapeDtypeStruct(full.shape, F32)],
        in_specs=[ANY] * 2,
        out_specs=[ANY] * 2,
        scratch_shapes=[vm(*out.shape), vm(*full.shape), dma(2, SHARES), dma(2, SHARES)],
        compiler_params=pltpu.CompilerParams(vmem_limit_bytes=VLIM * 1024 * 1024),
        name="hand_over",
    )(out, full)
    return out, full.reshape(probe.shape)


def solution(mesh):
    placed = (
        P(None, "row", "col"),
        P(),
        P("row", "col", None, None),
        P("row", "col"),
        P("row", "col", None, None, None),
    )
    return jax.shard_map(
        functools.partial(local, mesh.shape["row"], mesh.shape["col"]),
        mesh=mesh, in_specs=placed, out_specs=(P(None, "row", "col"), P()), check_vma=False)
```

```python
import functools
import math

import jax
import jax.numpy as jnp
import numpy as np
from jax import lax
from jax.experimental import pallas as pl
from jax.experimental.pallas import tpu as pltpu
from jax.sharding import PartitionSpec as P

MESH = pl.DeviceIdType.MESH
UNROLL = 8
VLIM = 60
PIECES = 8
SHARES = 4
RELEASE = (1, 1, 1, 1, 2, 1)
ANY = pl.BlockSpec(memory_space=pl.ANY)
VMEM = pl.BlockSpec(memory_space=pltpu.VMEM)
INSPEC = ANY
SMEM = pl.BlockSpec(memory_space=pltpu.SMEM)
F32 = jnp.float32
BF16 = jnp.bfloat16
N = 128
HALF = 64
SIDES = ((-1, 0), (1, 0), (0, -1), (0, 1), (-1, -1), (-1, 1), (1, -1), (1, 1))
OPPOSITE = tuple(SIDES.index((-a, -b)) for a, b in SIDES)


def neighbours(rows, cols):
    r, c = lax.axis_index("row"), lax.axis_index("col")
    out = []
    for dr, dc in SIDES:
        there = True
        if dr:
            there = (r > 0) if dr < 0 else (r < rows - 1)
        if dc:
            col_there = (c > 0) if dc < 0 else (c < cols - 1)
            there = col_there if there is True else jnp.logical_and(there, col_there)
        out.append((there, (r + dr, c + dc)))
    return out


def pack_low(tile):
    k = tile.shape[1] // 2
    lane = lax.broadcasted_iota(jnp.int32, (2, k, N), 2)
    return jnp.where(lane < HALF, tile[:, :k], pltpu.roll(tile[:, k:], HALF, 2))


def pack_high(tile):
    k = tile.shape[1] // 2
    lane = lax.broadcasted_iota(jnp.int32, (2, k, N), 2)
    return jnp.where(lane < HALF, pltpu.roll(tile[:, :k], HALF, 2), tile[:, k:])


def tables():
    ramp = np.arange(N)
    angles = 2.0 * math.pi / N * (ramp[:, None] * ramp[None, :] % N)
    cos, sin = np.cos(angles) / math.sqrt(N), np.sin(angles) / math.sqrt(N)
    minus = np.block([[cos, -sin], [sin, cos]]).astype(np.float32)
    return np.stack([minus, minus.T])


def each(count, body, unroll):
    def some(i, carry):
        body([i * unroll + k for k in range(unroll)])
        return carry

    lax.fori_loop(0, count // unroll, some, 0)


def split(x):
    high = x.astype(BF16)
    return high, (x - high.astype(F32)).astype(BF16)


def dot(a, b):
    return jnp.dot(a, b, preferred_element_type=F32)


def times_table(x, high, low):
    x_high, x_low = split(x)
    return dot(x_high, high) + (dot(x_low, high) + dot(x_high, low))


def table_times(high, low, x):
    x_high, x_low = split(x)
    both = dot(jnp.concatenate([high, low], axis=0), x_high)
    return both[:high.shape[0]] + (dot(high, x_low) + both[high.shape[0]:])


def peers():
    r, c = lax.axis_index("row"), lax.axis_index("col")
    y, z_hi = r // 4, r % 4
    x, z_lo, core = c // 4, c // 2 % 2, c % 2
    plane = [((y + k // 4) % 4 * 4 + z_hi, (x + k % 4) % 4 * 4 + c % 4) for k in range(1, 16)]
    z = z_hi * 2 + z_lo
    along_z = []
    for k in range(1, 8):
        other = (z + k) % 8
        along_z.append((y * 4 + other // 2, x * 4 + other % 2 * 2 + core))
    return x, y, z, core, plane, along_z, (r, c + 1 - 2 * core)


def remote(src, dst, send_sem, recv_sem, device):
    return pltpu.make_async_remote_copy(
        src_ref=src, dst_ref=dst, send_sem=send_sem, recv_sem=recv_sem, device_id=device, device_id_type=MESH)


def sum_everywhere(ring, total, full, from_core, in_xy, in_z, send_sem, recv_sem, scale):
    x, y, z, core, plane, along_z, sibling = ring
    rows = total.shape[0]
    half, piece = rows // 2, rows // 32
    mine = core * half
    own = mine + (y * 4 + x) * piece
    used = [0]

    def send(src, dst, device):
        i = used[0]
        used[0] += 1
        copy = remote(src, dst, send_sem.at[i], recv_sem.at[i], device)
        copy.start()
        return copy

    def finish(copies):
        for copy in copies:
            copy.wait()

    span = lambda start, count: pl.ds(pl.multiple_of(start, 8), count)
    at = lambda ref, start, count: ref.at[span(start, count), :]

    def steps():
        copies = [send(at(total, half - mine, half), from_core, sibling)]
        yield
        finish(copies)
        total[span(mine, half), :] += from_core[...]
        copies = [send(at(total, mine + ((y + k // 4) % 4 * 4 + (x + k % 4) % 4) * piece, piece), in_xy.at[k - 1],
                       plane[k - 1]) for k in range(1, 16)]
        yield
        finish(copies)
        in_z[z] = total[span(own, piece), :] + sum(in_xy[k] for k in range(15))
        copies = [send(in_z.at[z], in_z.at[z], device) for device in along_z]
        yield
        finish(copies)
        full[span(own, piece), :] = sum(in_z[k] for k in range(8)) * scale
        copies = [send(at(full, own, piece), at(full, own, piece), device) for device in plane]
        yield
        finish(copies)
        copies = [send(at(full, mine, half), at(full, mine, half), sibling)]
        yield
        finish(copies)
        yield

    run = steps()
    return lambda: next(run)


def spread(x, k):
    return x, pltpu.roll(x, HALF, 2)


def turn_lanes(x, by):
    lane = lax.broadcasted_iota(jnp.int32, (8 * x.shape[0], N), 1)
    return jnp.take_along_axis(x.reshape(-1, N), (lane + (N - by)) & (N - 1), axis=1).reshape(x.shape)


def turn_rows(x, by):
    index = (lax.broadcasted_iota(jnp.int32, (8, N), 0) + (8 - by)) & 7
    return jnp.stack([jnp.take_along_axis(x[k], index, axis=0) for k in range(x.shape[0])])


def kernel(rows, cols, scale, pos_in, count_in, obj, probe_in, measured_in, table_in, out, full,
           pos, count, ext, field, probe, measured, table_whole, table, patches, mids, sums, strips, strips_in, corners, corners_in,
           moved, rim_sides, rim_corners, land_up, land_down, land_sides, land_corners,
           total, from_core, in_xy, in_z, load_sem, halo_send, halo_recv, rim_send, rim_recv, send_sem, recv_sem):
    modes, slots = probe.shape[0], measured.shape[0]
    size = out.shape[1]
    tiles = size // N + 2
    edge, far_edge = HALF // 8, (HALF + size) // 8
    groups = N // 8
    near = neighbours(rows, cols)

    loads = [pltpu.make_async_copy(a, b, load_sem.at[i]) for i, (a, b) in enumerate((
        (obj, ext.at[:, pl.ds(edge, size // 8), :, pl.ds(N, size)]),
        (pos_in, pos), (count_in, count), (probe_in, probe), (measured_in, measured), (table_in, table_whole)))]
    for load in loads:
        load.start()

    barrier = pltpu.get_barrier_semaphore()
    ring = peers()
    others = ring[-3] + ring[-2] + [ring[-1]]
    for device in others:
        pl.semaphore_signal(barrier, inc=1, device_id=device, device_id_type=MESH)
    for there, device in near:
        @pl.when(there)
        def _():
            pl.semaphore_signal(barrier, inc=1, device_id=device, device_id_type=MESH)
    pl.semaphore_wait(barrier, len(others) + sum(there.astype(jnp.int32) for there, _ in near))

    sources = [obj.at[:, pl.ds(0, edge)], obj.at[:, pl.ds(size // 8 - edge, edge)],
               strips.at[0], strips.at[1]] + [corners.at[i] for i in range(4)]
    landing = [ext.at[:, pl.ds(0, edge), :, pl.ds(N, size)], ext.at[:, pl.ds(far_edge, edge), :, pl.ds(N, size)],
               strips_in.at[0], strips_in.at[1]] + [corners_in.at[i] for i in range(4)]
    halo = [remote(sources[i], landing[OPPOSITE[i]], halo_send.at[i], halo_recv.at[OPPOSITE[i]], near[i][1])
            for i in range(8)]

    def start(copies, side):
        @pl.when(near[side][0])
        def _():
            copies[side].start()

    start(halo, 0)
    start(halo, 1)
    loads[0].wait()
    first_tile = ext[:, edge:far_edge, :, N:2 * N].reshape(2, size, N)
    last_tile = ext[:, edge:far_edge, :, size:size + N].reshape(2, size, N)
    strips[0] = pack_low(first_tile)
    start(halo, 2)
    strips[1] = pack_high(last_tile)
    start(halo, 3)
    corners[0] = pack_low(first_tile[:, :HALF])
    corners[1] = pack_high(last_tile[:, :HALF])
    corners[2] = pack_low(first_tile[:, size - HALF:])
    corners[3] = pack_high(last_tile[:, size - HALF:])
    for side in range(4, 8):
        start(halo, side)
    total[...] = jnp.zeros_like(total)
    for g in (0, groups + 2):
        moved[:, :, g] = jnp.zeros((slots, 2, 8, size + 2 * N), F32)
    for load in loads[1:]:
        load.wait()
    table[0], table[1] = split(table_whole[0])
    table[2], table[3] = split(table_whole[1])
    for side in range(8):
        @pl.when(jnp.logical_not(near[side][0]))
        def _():
            landing[side][...] = jnp.zeros(landing[side].shape, F32)
    for t in range(1, tiles - 1):
        field[:, t, edge:far_edge] = ext[:, edge:far_edge, :, t * N:(t + 1) * N]
    for side in range(8):
        @pl.when(near[side][0])
        def _():
            halo[side].wait_send()
            halo[OPPOSITE[side]].wait_recv()

    def unpack(packed, at, lane, is_low):
        k = packed.shape[1] // 8
        as_is, turned = spread(packed, k)
        first, second = (as_is, turned) if is_low else (turned, as_is)
        field[:, lane // N, at:at + k] = first.reshape(2, k, 8, N)
        field[:, lane // N, at + k:at + 2 * k] = second.reshape(2, k, 8, N)

    unpack(strips_in[0], edge, 0, False)
    unpack(strips_in[1], edge, N + size, True)
    unpack(corners_in[0], 0, 0, False)
    unpack(corners_in[1], 0, N + size, True)
    unpack(corners_in[2], far_edge, 0, False)
    unpack(corners_in[3], far_edge, N + size, True)

    for t in range(1, tiles - 1):
        field[:, t, :edge] = ext[:, :edge, :, t * N:(t + 1) * N]
        field[:, t, far_edge:] = ext[:, far_edge:, :, t * N:(t + 1) * N]

    minus_high, minus_low, plus_high, plus_low = (table[i] for i in range(4))
    lane = lax.broadcasted_iota(jnp.int32, (groups + 1, 8, N), 2)
    step = lax.broadcasted_iota(jnp.int32, (groups + 1, 8, N), 1)
    live = count[0, 0]

    def place(slot):
        row, col = pos[0, slot], pos[1, slot] + HALF
        return row // 8, row % 8, col // N, col % N

    def waves_of(slot):
        group, down_by, tile, shift = place(slot)
        kept = lane >= shift

        def cut(part):
            a, b = (jnp.stack([field[part, tile + t, group + k] for k in range(groups + 1)]) for t in (0, 1))
            x = turn_lanes(jnp.where(kept, a, b), N - shift)
            x = turn_rows(x, 8 - down_by)
            return jnp.where(step[:groups] < 8 - down_by, x[:groups], x[1:]).reshape(N, N)

        p_re, p_im = cut(0), cut(1)
        patches[slot, 0] = p_re
        patches[slot, 1] = p_im
        waves = []
        for m in range(modes):
            q_re, q_im = probe[m, 0], probe[m, 1]
            waves.append(jnp.concatenate([q_re * p_re - q_im * p_im, q_re * p_im + q_im * p_re], axis=1))
        return waves

    def first_steps(some):
        half = times_table(jnp.concatenate(sum((waves_of(slot) for slot in some), []), axis=0), minus_high, minus_low)
        for k, slot in enumerate(some):
            along_rows(slot, half[k * modes * N:(k + 1) * modes * N])

    def along_rows(slot, half):
        half = jnp.concatenate(
            [jnp.concatenate([half[m * N:(m + 1) * N, :N], half[m * N:(m + 1) * N, N:]], axis=0)
             for m in range(modes)], axis=1)
        far = table_times(plus_high, plus_low, half)
        power = far[:N] * far[:N] + far[N:] * far[N:]
        intensity = sum(power[:, m * N:(m + 1) * N] for m in range(modes))
        alive = jnp.where(slot < live, 1.0, 0.0).astype(F32)
        factor = (1.0 - measured[slot] * lax.rsqrt(intensity + 0.1)) * alive
        wide = jnp.concatenate([factor] * modes, axis=1)
        far = far * jnp.concatenate([wide, wide], axis=0)
        half = table_times(minus_high, minus_low, far)
        for m in range(modes):
            mids[slot, m, :, :N] = half[:N, m * N:(m + 1) * N]
            mids[slot, m, :, N:] = half[N:, m * N:(m + 1) * N]

    each(slots, first_steps, UNROLL)

    def last_step(slots_now, some):
        height = len(some) * N
        x = [mids[slot, some[0]:some[-1] + 1].reshape(height, 2 * N) for slot in slots_now]
        g_all = times_table(jnp.concatenate(x, axis=0), plus_high, plus_low)
        result = []
        for i, slot in enumerate(slots_now):
            g = g_all[i * height:(i + 1) * height]
            p_re, p_im = patches[slot, 0], patches[slot, 1]
            o_re = jnp.zeros((N, N), F32)
            o_im = jnp.zeros((N, N), F32)
            for k, m in enumerate(some):
                g_re, g_im = g[k * N:(k + 1) * N, :N], g[k * N:(k + 1) * N, N:]
                q_re, q_im = probe[m, 0], probe[m, 1]
                o_re += q_re * g_re + q_im * g_im
                o_im += q_re * g_im - q_im * g_re
                total[2 * m * N:(2 * m + 1) * N] += p_re * g_re + p_im * g_im
                total[(2 * m + 1) * N:(2 * m + 2) * N] += p_re * g_im - p_im * g_re
            result.append((o_re, o_im))
        return result

    def first_modes(some):
        for slot, (o_re, o_im) in zip(some, last_step(some, early)):
            sums[slot, 0], sums[slot, 1] = o_re, o_im

    def last_modes(some):
        for slot, (o_re, o_im) in zip(some, last_step(some, late)):
            _, down_by, tile, shift = place(slot)
            blank = jnp.zeros((1, 8, N), F32)
            for part, value in ((0, sums[slot, 0] + o_re), (1, sums[slot, 1] + o_im)):
                x = turn_lanes(value.reshape(groups, 8, N), shift)
                x = turn_rows(x, down_by)
                x = jnp.where(step >= down_by, jnp.concatenate([x, blank]), jnp.concatenate([blank, x]))
                for t in range(tiles):
                    from_start = lane[:1] + (t * N - shift) - tile * N
                    inside = jnp.logical_and(from_start >= 0, from_start < N)
                    moved[slot, part, 1:groups + 2, :, t * N:(t + 1) * N] = jnp.where(inside, x, 0.0)

    early, late = tuple(range(modes // 2)), tuple(range(modes // 2, modes))
    cut_at = 2 * len(early) * N
    advance_a, advance_b = (
        sum_everywhere(ring, total.at[rows_of], full.at[rows_of], from_core.at[i], in_xy.at[i], in_z.at[i],
                       send_sem.at[i], recv_sem.at[i], scale)
        for i, rows_of in enumerate((pl.ds(0, cut_at), pl.ds(cut_at, total.shape[0] - cut_at))))
    each(slots, first_modes, UNROLL)
    advance_a()
    each(slots, last_modes, UNROLL)
    advance_a()
    advance_b()
    starts = [place(slot)[0] for slot in range(slots)]

    def gather(some):
        g, = some
        at = [jnp.clip(g - start + 1, 0, groups + 2) for start in starts]
        for part in (0, 1):
            ext[part, g] = sum(moved[slot, part, at[slot]] for slot in range(slots))

    each(ext.shape[1], gather, 1)
    advance_b()
    block = lambda at, k, lane: ext[:, at:at + k, :, lane:lane + N].reshape(2, 8 * k, N)
    rim_sides[0] = pack_high(block(edge, size // 8, 0))
    rim_sides[1] = pack_low(block(edge, size // 8, N + size))
    rim_corners[0] = pack_high(block(0, edge, 0))
    rim_corners[1] = pack_low(block(0, edge, N + size))
    rim_corners[2] = pack_high(block(far_edge, edge, 0))
    rim_corners[3] = pack_low(block(far_edge, edge, N + size))

    per_row, per_side = edge // PIECES, size // 2 // PIECES
    rims = []
    for p in range(PIECES):
        rows_of, part_of = pl.ds(p * per_row, per_row), pl.ds(p * per_side, per_side)
        rims.append([
            (0, ext.at[:, rows_of, :, pl.ds(N, size)], land_down.at[:, rows_of]),
            (1, ext.at[:, pl.ds(far_edge + p * per_row, per_row), :, pl.ds(N, size)], land_up.at[:, rows_of]),
            (2, rim_sides.at[0, :, part_of], land_sides.at[1, :, part_of]),
            (3, rim_sides.at[1, :, part_of], land_sides.at[0, :, part_of])])
    for i in range(4):
        rims[i * PIECES // 4].append((4 + i, rim_corners.at[i], land_corners.at[OPPOSITE[4 + i] - 4]))
    rims = [[(side, remote(src, dst, rim_send.at[p, side], rim_recv.at[p, OPPOSITE[side]], near[side][1]))
             for side, src, dst in piece] for p, piece in enumerate(rims)]
    left = list(rims)

    def release(count):
        for _ in range(min(count, len(left))):
            for side, copy in left.pop(0):
                @pl.when(near[side][0])
                def _():
                    copy.start()

    release(RELEASE[0])
    advance_a()
    release(RELEASE[1])
    out[...] = ext[:, edge:far_edge, :, N:N + size].reshape(2, size, size)
    advance_b()
    release(RELEASE[2])
    advance_a()
    release(RELEASE[3])
    advance_b()
    release(RELEASE[4])
    advance_a()
    release(RELEASE[5])
    advance_b()
    release(PIECES)
    advance_a()
    advance_b()

    def add(packed, row, is_low):
        k = packed.shape[1]
        lane_of = lax.broadcasted_iota(jnp.int32, (2, k, N), 2)
        as_is, turned = spread(packed, k)
        first, second = (as_is, turned) if is_low else (turned, as_is)
        inside = (lane_of < HALF) if is_low else (lane_of >= HALF)
        at = 0 if is_low else size - N
        out[:, row:row + k, at:at + N] += jnp.where(inside, first, 0.0)
        out[:, row + k:row + 2 * k, at:at + N] += jnp.where(inside, second, 0.0)

    for piece in rims:
        for side, copy in piece:
            @pl.when(near[side][0])
            def _():
                copy.wait_send()

            @pl.when(near[OPPOSITE[side]][0])
            def _():
                copy.wait_recv()

    for side in range(8):
        @pl.when(near[side][0])
        def _():
            if side == 0:
                out[:, :HALF, :] += land_up[...].reshape(2, HALF, size)
            elif side == 1:
                out[:, size - HALF:, :] += land_down[...].reshape(2, HALF, size)
            elif side < 4:
                add(land_sides[side - 2], 0, side == 2)
            else:
                add(land_corners[side - 4], 0 if side < 6 else size - HALF, side in (4, 6))


def hand_over_kernel(a, b, out_a, out_b, held_a, held_b, load_sem, store_sem):
    part_a, part_b = a.shape[1] // SHARES, b.shape[0] // SHARES
    loads, stores = [], []
    for i in range(SHARES):
        rows_a, rows_b = pl.ds(i * part_a, part_a), pl.ds(i * part_b, part_b)
        loads.append(pltpu.make_async_copy(a.at[:, rows_a], held_a.at[:, rows_a], load_sem.at[0, i]))
        loads.append(pltpu.make_async_copy(b.at[rows_b], held_b.at[rows_b], load_sem.at[1, i]))
        stores.append(pltpu.make_async_copy(held_a.at[:, rows_a], out_a.at[:, rows_a], store_sem.at[0, i]))
        stores.append(pltpu.make_async_copy(held_b.at[rows_b], out_b.at[rows_b], store_sem.at[1, i]))
    for load in loads:
        load.start()
    for load, store in zip(loads, stores):
        load.wait()
        store.start()
    for store in stores:
        store.wait()


def local(rows, cols, object_field, probe, positions, counts, measured):
    size = object_field.shape[1]
    slots, modes = measured.shape[2], probe.shape[0]
    scale = 1.0 / math.sqrt(rows * cols * slots)
    height = 2 * modes * N
    vm = lambda *dims: pltpu.VMEM(dims, F32)
    dma = lambda *count: pltpu.SemaphoreType.DMA(count)
    strip, side, corner = (2, HALF // 8, 8, size), (2, 2, size // 2, N), (4, 2, HALF // 2, N)
    out, full = pl.pallas_call(
        functools.partial(kernel, rows, cols, scale),
        out_shape=[jax.ShapeDtypeStruct(object_field.shape, F32), jax.ShapeDtypeStruct((height, N), F32)],
        in_specs=[INSPEC] * 6,
        out_specs=[VMEM] * 2,
        scratch_shapes=[
            pltpu.SMEM((2, slots), jnp.int32), pltpu.SMEM(counts.shape, jnp.int32),
            vm(2, (size + N) // 8, 8, size + 2 * N), vm(2, size // N + 2, (size + N) // 8, 8, N), vm(*probe.shape), vm(slots, N, N),
            vm(2, 2 * N, 2 * N), pltpu.VMEM((4, 2 * N, 2 * N), BF16),
            vm(slots, 2, N, N), vm(slots, modes, N, 2 * N), vm(slots, 2, N, N),
            vm(*side), vm(*side), vm(*corner), vm(*corner),
            vm(slots, 2, N // 8 + 3, 8, size + 2 * N),
            vm(*side), vm(*corner),
            vm(*strip), vm(*strip), vm(*side), vm(*corner),
            vm(height, N), vm(2, height // 4, N), vm(2, 15, height // 64, N), vm(2, 8, height // 64, N),
            dma(6), dma(8), dma(8), dma(PIECES, 8), dma(PIECES, 8), dma(2, 39), dma(2, 39),
        ],
        compiler_params=pltpu.CompilerParams(
            collective_id=0, has_side_effects=True, vmem_limit_bytes=VLIM * 1024 * 1024),
        name="step",
    )(positions[0, 0].T, counts, object_field.reshape(2, size // 8, 8, size), probe, measured[0, 0], jnp.asarray(tables()))
    out, full = pl.pallas_call(
        hand_over_kernel,
        out_shape=[jax.ShapeDtypeStruct(out.shape, F32), jax.ShapeDtypeStruct(full.shape, F32)],
        in_specs=[ANY] * 2,
        out_specs=[ANY] * 2,
        scratch_shapes=[vm(*out.shape), vm(*full.shape), dma(2, SHARES), dma(2, SHARES)],
        compiler_params=pltpu.CompilerParams(vmem_limit_bytes=VLIM * 1024 * 1024),
        name="hand_over",
    )(out, full)
    return out, full.reshape(probe.shape)


def solution(mesh):
    placed = (
        P(None, "row", "col"),
        P(),
        P("row", "col", None, None),
        P("row", "col"),
        P("row", "col", None, None, None),
    )
    return jax.shard_map(
        functools.partial(local, mesh.shape["row"], mesh.shape["col"]),
        mesh=mesh, in_specs=placed, out_specs=(P(None, "row", "col"), P()), check_vma=False)
```
